32 devices in a mesh: grp: 2 (over x), ep: 16 (over z, y, core).
Axes of the slice: x: 2, y: 2, z: 4, core: 2. Of those that a mesh axis runs over, the one named last changes fastest.
Arguments:
- tokens: bfloat16 [4096, 512], P(('grp', 'ep')), may hold values from -6 to 6
- teacher: bfloat16 [4096, 7168], P(('grp', 'ep')), may hold values from -6 to 6
- expert_ids: int32 [4096, 4], P(('grp', 'ep')), may hold values from 0 to 15, all different within a row; in each aligned block of 128 rows (0 to 127, 128 to 255, ...) at most 48 rows name the same one
- route_weights: float32 [4096, 4], P(('grp', 'ep')), may hold values from 0.1 to 1
- w_gate: bfloat16 [16, 512, 1024], P('ep', 'grp'), may hold values from -0.25 to 0.25
- w_up: bfloat16 [16, 512, 1024], P('ep', 'grp'), may hold values from -0.25 to 0.25
- w_down: bfloat16 [16, 1024, 512], P('ep', 'grp'), may hold values from -0.1875 to 0.1875
- critic_teacher: bfloat16 [7168, 512], P('ep'), may hold values from -0.0625 to 0.0625
- critic_student: bfloat16 [512, 512], P('ep'), may hold values from -0.25 to 0.25
- critic_head: float32 [512], replicated, may hold values from -0.25 to 0.25
Outputs:
- grad_gate: float32 [16, 512, 1024], P('ep', 'grp')
- grad_up: float32 [16, 512, 1024], P('ep', 'grp')
- grad_down: float32 [16, 1024, 512], P('ep', 'grp')
- scores: float32 [4096], P(('grp', 'ep'))
The draws below stay inside these ranges and needn't reach their ends.
Inputs may be any that keep to these rules, and one draw needn't show every extreme that they name: `expert_ids`: each row names 4 different experts. Among the 128 rows of one device no expert is named more than 48 times, and in every draw some expert is named exactly 48 times by the rows of some device.
All inputs are finite; a program needn't handle non-finite values.
Results may differ from the reference program's by a relative error of at most 0.013.
Values may be sent and summed in bfloat16 or wider, within the bound.
A program may use at most 64 MiB of HBM per device.

```python
import math
import jax
import jax.numpy as jnp
import numpy as np
from jax import lax

D = 512
H = 1024
DT = 7168
K = 512
TOP = 4
TOK_DEV = 128
EXPERTS = 16
CAP = 48
TOKENS = 4096
N_GRP = 2
N_EP = 16


def block_scale(key, extent, cuts, smallest, largest):
    def one(axis_at, shards_of):
        draws = jax.random.uniform(jax.random.fold_in(jax.random.fold_in(key, 6), axis_at), (shards_of,), jnp.float32, smallest / len(cuts), largest / len(cuts))
        return jnp.repeat(jnp.exp(draws), extent[axis_at] // shards_of).reshape((-1,) + (1,) * (len(extent) - axis_at - 1))

    level = one(*cuts[0])
    for cut in cuts[1:]:
        level = level * one(*cut)
    return level


def deal_out(stream_key, own, number, rows, number_of, top, most, lean):
    sequence = jax.random.permutation(stream_key, number_of)
    heavy_load, common = shares(number_of, rows * top, most, lean, True), shares(number_of, rows * top, most, lean, False)
    places = jnp.arange(number_of)

    def named(lengths, turn):
        used = int((lengths > 0).sum())
        fixed = max(1, used // 4)
        passed = fixed + (places - fixed + turn * (used - fixed)) % max(1, number_of - fixed)
        return jnp.zeros((number_of,), jnp.int32).at[sequence[jnp.where(places < fixed, places, passed)]].set(jnp.asarray(lengths, jnp.int32))

    lengths = jnp.where(number % 4 == 0, named(heavy_load, number // 4), named(common, number - number // 4 - 1))
    mixed = jax.random.permutation(jax.random.fold_in(own, 3), number_of)
    source_of, receiver = mixed[0:number_of // 2 * 2:2], mixed[1:number_of // 2 * 2:2]
    room = jnp.minimum(lengths[source_of] - 1, most - lengths[receiver]) // 2
    room = jnp.where((source_of == sequence[0]) | (receiver == sequence[0]) | (lengths[receiver] == 0), 0, jnp.maximum(room, 0))
    passed = jax.random.randint(jax.random.fold_in(own, 4), (number_of // 2,), 0, 1 << 20) % (room + 1)
    lengths = lengths.at[source_of].add(-passed).at[receiver].add(passed)
    items = jnp.searchsorted(jnp.cumsum(lengths), jnp.arange(rows * top), side="right").astype(jnp.int32)
    table = items.reshape(top, rows).T
    table = table[jax.random.permutation(jax.random.fold_in(own, 1), rows)]
    turn = jax.random.randint(jax.random.fold_in(own, 2), (rows, 1), 0, top)
    return jnp.take_along_axis(table, (jnp.arange(top)[None, :] + turn) % top, axis=1)


def shares(amount, total, reach, skew, full):
    loads = [(1 << 20) // math.isqrt(rank ** skew) + 1 for rank in range(1, amount + 1)]
    largest = reach if full else min(reach, max(-(-total // amount), total * loads[0] // sum(loads)))
    least = 1 if total - largest >= amount - 1 else 0
    counts, surplus = [largest] + [least] * (amount - 1), total - largest - least * (amount - 1)
    while surplus > 0:
        free = [i for i in range(1, amount) if counts[i] < largest] or [i for i in range(1, amount) if counts[i] < reach]
        whole, left = sum([loads[i] for i in free]), surplus
        for i in free:
            extra = min(reach - counts[i], max(1, left * loads[i] // whole), surplus)
            counts[i] = counts[i] + extra
            surplus = surplus - extra
    return np.array(counts)


def scatter_about(rng, dims, scale, limit, shards=(), kind=jnp.bfloat16):
    entries = jax.random.normal(rng, dims, jnp.float32) * scale
    if len(shards) > 0:
        entries = block_scale(rng, dims, shards, -0.22, 0.18) * entries
    return jnp.clip(entries, min=-limit, max=limit).astype(kind)


def setup_inputs(seed: int = 0) -> dict:
    splits = jax.random.split(jax.random.key(seed), 11)
    tokens = scatter_about(splits[0], (TOKENS, D), 1.0, 6.0, ((0, 32),))
    teacher = scatter_about(splits[1], (TOKENS, DT), 1.0, 6.0, ((0, 32),))
    expert_ids_keys = jax.random.split(jax.random.fold_in(splits[2], 1), TOKENS // TOK_DEV)
    expert_ids_turns = jax.random.permutation(jax.random.fold_in(splits[2], 3), TOKENS // TOK_DEV)
    expert_ids = jax.vmap(lambda own, number: deal_out(jax.random.fold_in(splits[2], 2), own, number, TOK_DEV, EXPERTS, TOP, CAP, 2))(expert_ids_keys, expert_ids_turns).reshape((TOKENS, TOP))
    route_weights = jnp.clip(jnp.exp(math.log(1.0) - 2.3025851 * jax.random.uniform(splits[3], (TOKENS, TOP), jnp.float32) ** block_scale(splits[3], (TOKENS, TOP), ((0, 32),), -0.2, 0.2)), 0.1, 1.0)
    w_gate = scatter_about(splits[4], (EXPERTS, D, H), D ** -0.5, 0.25, ((0, 16), (1, 2)))
    w_up = scatter_about(splits[5], (EXPERTS, D, H), D ** -0.5, 0.25, ((0, 16), (1, 2)))
    w_down = scatter_about(splits[6], (EXPERTS, H, D), H ** -0.5, 0.1875, ((0, 16), (1, 2)))
    critic_teacher = scatter_about(splits[7], (DT, K), DT ** -0.5, 0.0625, ((0, 16),))
    critic_student = scatter_about(splits[8], (D, K), D ** -0.5, 0.25, ((0, 16),))
    critic_head = scatter_about(splits[9], (K,), K ** -0.5, 0.25, (), jnp.float32)
    return {"tokens": tokens, "teacher": teacher, "expert_ids": expert_ids, "route_weights": route_weights, "w_gate": w_gate, "w_up": w_up, "w_down": w_down, "critic_teacher": critic_teacher, "critic_student": critic_student, "critic_head": critic_head}


def gelu_tanh(value):
    inner = 0.7978845608 * (value + 0.044715 * value * value * value)
    return 0.5 * value * (1.0 + jnp.tanh(inner))


def gelu_slope(value):
    inner = 0.7978845608 * (value + 0.044715 * value * value * value)
    tangent = jnp.tanh(inner)
    return 0.5 * (1.0 + tangent) + 0.5 * value * (1.0 - tangent * tangent) * 0.7978845608 * (1.0 + 3.0 * 0.044715 * value * value)


def slots_of(ids):
    flat = ids.reshape(-1).astype(jnp.int32)
    onehot = (flat[:, None] == jnp.arange(EXPERTS, dtype=jnp.int32)[None, :]).astype(jnp.int32)
    before = jnp.cumsum(onehot, axis=0) - onehot
    return (flat * CAP + jnp.sum(before * onehot, axis=1)).astype(jnp.int32)


def place(slots, rows):
    return jnp.zeros((EXPERTS * CAP, rows.shape[-1]), rows.dtype).at[slots].set(rows)


def to_experts(buffer):
    return buffer.reshape(N_EP, EXPERTS, CAP, D).transpose(1, 0, 2, 3).reshape(EXPERTS, N_EP * CAP, D)


def from_experts(buffer):
    return buffer.reshape(EXPERTS, N_EP, CAP, D).transpose(1, 0, 2, 3).reshape(N_EP, EXPERTS * CAP, D)


def rounded(value):
    low = lax.optimization_barrier(value.astype(jnp.bfloat16))
    return low.astype(jnp.float32)


def reference(tokens, teacher, expert_ids, route_weights, w_gate, w_up, w_down, critic_teacher, critic_student, critic_head):
    rows = N_EP * TOK_DEV
    wg32 = w_gate.astype(jnp.float32)
    wu32 = w_up.astype(jnp.float32)
    wd32 = w_down.astype(jnp.float32)
    items = (tokens.reshape(N_GRP, N_EP, TOK_DEV, D),
             teacher.reshape(N_GRP, rows, DT),
             expert_ids.reshape(N_GRP, N_EP, TOK_DEV * TOP),
             route_weights.reshape(N_GRP, N_EP, TOK_DEV, TOP))

    def group_step(carry, item):
        acc_gate, acc_up, acc_down = carry
        xs, feats, ids, weights = item
        slots = jax.vmap(slots_of)(ids)
        spread = jnp.repeat(xs, TOP, axis=1)
        routed = to_experts(jax.vmap(place)(slots, spread))
        routed32 = routed.astype(jnp.float32)
        gate = jnp.einsum("erd,edh->erh", routed32, wg32)
        up = jnp.einsum("erd,edh->erh", routed32, wu32)
        hidden = (jax.nn.silu(gate) * up).astype(jnp.bfloat16)
        hidden32 = hidden.astype(jnp.float32)
        expert_out = jnp.einsum("erh,ehd->erd", hidden32, wd32).astype(jnp.bfloat16)
        back = from_experts(expert_out)
        picked = jax.vmap(lambda buf, sl: buf[sl])(back, slots).reshape(N_EP, TOK_DEV, TOP, D)
        student = jnp.sum(picked.astype(jnp.float32) * weights[..., None], axis=2).astype(jnp.bfloat16)
        student = student.reshape(rows, D)
        pre = jnp.dot(feats, critic_teacher, preferred_element_type=jnp.float32) + jnp.dot(student, critic_student, preferred_element_type=jnp.float32)
        score = jnp.sum(gelu_tanh(pre) * critic_head[None, :], axis=1)
        dscore = -jax.nn.sigmoid(-score)
        dpre = (dscore[:, None] * critic_head[None, :] * gelu_slope(pre)).astype(jnp.bfloat16)
        dstudent = jnp.dot(dpre, critic_student.T, preferred_element_type=jnp.float32).reshape(N_EP, TOK_DEV, 1, D)
        dassign = (weights[..., None] * dstudent).astype(jnp.bfloat16).reshape(N_EP, TOK_DEV * TOP, D)
        droute = to_experts(jax.vmap(place)(slots, dassign)).astype(jnp.float32)
        dhidden = jnp.einsum("erd,ehd->erh", droute, wd32)
        sig = jax.nn.sigmoid(gate)
        dgate = (dhidden * up * sig * (1.0 + gate * (1.0 - sig))).astype(jnp.bfloat16).astype(jnp.float32)
        dup = (dhidden * gate * sig).astype(jnp.bfloat16).astype(jnp.float32)
        part_gate = jnp.einsum("erd,erh->edh", routed32, dgate)
        part_up = jnp.einsum("erd,erh->edh", routed32, dup)
        part_down = jnp.einsum("erh,erd->ehd", hidden32, droute)
        carry = (acc_gate + rounded(part_gate), acc_up + rounded(part_up), acc_down + rounded(part_down))
        return carry, score

    start = (jnp.zeros((EXPERTS, D, H), jnp.float32), jnp.zeros((EXPERTS, D, H), jnp.float32), jnp.zeros((EXPERTS, H, D), jnp.float32))
    sums, scores = lax.scan(group_step, start, items)
    return sums[0], sums[1], sums[2], scores.reshape(TOKENS)
```

```python
import functools

import jax
import jax.numpy as jnp
from jax import lax
from jax.experimental import pallas as pl
from jax.experimental.pallas import tpu as pltpu
from jax.sharding import PartitionSpec as P

BF = jnp.bfloat16
F32 = jnp.float32
MESH = pl.DeviceIdType.MESH


def gelu_tanh(value):
    inner = 0.7978845608 * (value + 0.044715 * value * value * value)
    return 0.5 * value * (1.0 + jnp.tanh(inner))


def gelu_slope(value):
    inner = 0.7978845608 * (value + 0.044715 * value * value * value)
    tangent = jnp.tanh(inner)
    return 0.5 * (1.0 + tangent) + 0.5 * value * (1.0 - tangent * tangent) * 0.7978845608 * (
        1.0 + 3.0 * 0.044715 * value * value
    )


def dot(left, right):
    return jnp.dot(left, right, preferred_element_type=F32)


def contract_rows(left, right):
    return lax.dot_general(left, right, (((0,), (0,)), ((), ())), preferred_element_type=F32)


def contract_cols(left, right):
    return lax.dot_general(left, right, (((1,), (1,)), ((), ())), preferred_element_type=F32)


def split(value):
    high = value.astype(BF)
    return high, (value - high.astype(F32)).astype(BF)


def sigmoid(v):
    return 0.5 * jnp.tanh(0.5 * v) + 0.5


def kernel(
    ng,
    ne,
    na,
    nb,
    cap,
    rs,
    tok_ref,
    tea_ref,
    ids_ref,
    rw_ref,
    wg_ref,
    wu_ref,
    wd_ref,
    ct_ref,
    cs_ref,
    ch_ref,
    gg_ref,
    gu_ref,
    gd_ref,
    sc_ref,
    ct,
    cs,
    wg,
    wu,
    wd,
    outb,
    routed,
    gate,
    up,
    hid,
    eout,
    back,
    gout,
    drt,
    dg,
    du,
    pg,
    pu,
    pd,
    rg,
    ru,
    rd,
    onehot,
    wslot,
    pre,
    s_disp,
    r_disp,
    s_ret,
    r_ret,
    s_dr,
    r_dr,
    s_w,
    r_w,
    s_g,
    r_g,
    r_c,
    s_c1,
    s_c2,
    s_c3,
):
    g = lax.axis_index("grp")
    e = lax.axis_index("ep")
    core = lax.rem(e, 2)
    bb = lax.rem(e // 2, nb)
    aa = e // (2 * nb)
    rows = ne * cap
    tok = tok_ref.shape[0]
    rt = ct_ref.shape[0]

    barrier = pltpu.get_barrier_semaphore()

    def greet(d, carry):
        pl.semaphore_signal(
            barrier, inc=1, device_id=(g, lax.rem(e + d, ne)), device_id_type=MESH
        )
        return carry

    lax.fori_loop(1, ne, greet, 0)

    def greet_g(d, carry):
        pl.semaphore_signal(
            barrier, inc=1, device_id=(lax.rem(g + d, ng), e), device_id_type=MESH
        )
        return carry

    lax.fori_loop(1, ng, greet_g, 0)

    row_e = lax.broadcasted_iota(jnp.int32, (ne, tok), 0)
    member = jnp.zeros((ne, tok), F32)
    weight = jnp.zeros((ne, tok), F32)
    for k in range(ids_ref.shape[0]):
        hit = ids_ref[k : k + 1, :] == row_e
        member = jnp.where(hit, 1.0, member)
        weight = jnp.where(hit, rw_ref[k : k + 1, :], weight)
    earlier = (
        lax.broadcasted_iota(jnp.int32, (tok, tok), 0)
        < lax.broadcasted_iota(jnp.int32, (tok, tok), 1)
    ).astype(F32)
    rank = dot(member.astype(BF), earlier.astype(BF))
    rank = jnp.where(member > 0.5, rank, -1.0)
    place = lax.broadcasted_iota(jnp.int32, (ne, cap, tok), 1).astype(F32)
    at = rank[:, None, :] == place
    onehot[...] = jnp.where(at, 1.0, 0.0).reshape(rows, tok).astype(BF)
    wslot[...] = jnp.where(at, weight[:, None, :], 0.0).reshape(rows, tok)
    outb[...] = dot(onehot[...], tok_ref[...]).astype(BF)

    def slots_of(d):
        return pl.ds(pl.multiple_of(d * cap, 16), cap)

    def exchange(src, dst, send, recv, peer):
        return pltpu.make_async_remote_copy(
            src_ref=src.at[slots_of(peer)],
            dst_ref=dst.at[slots_of(e)],
            send_sem=send.at[peer],
            recv_sem=recv.at[e],
            device_id=(g, peer),
            device_id_type=MESH,
        )

    def arrival(src, dst, send, recv, peer):
        return pltpu.make_async_remote_copy(
            src_ref=src.at[slots_of(e)],
            dst_ref=dst.at[slots_of(peer)],
            send_sem=send.at[peer],
            recv_sem=recv.at[peer],
            device_id=(g, peer),
            device_id_type=MESH,
        )

    def send_all(src, dst, send, recv):
        def one(d, carry):
            exchange(src, dst, send, recv, lax.rem(e + d, ne)).start()
            return carry

        lax.fori_loop(1, ne, one, 0)
        dst[slots_of(e), :] = src[slots_of(e), :]

    def take_all(src, dst, send, recv):
        def one(d, carry):
            arrival(src, dst, send, recv, lax.rem(e + ne - d, ne)).wait_recv()
            return carry

        lax.fori_loop(1, ne, one, 0)

    def sent_all(src, dst, send, recv):
        def one(d, carry):
            exchange(src, dst, send, recv, lax.rem(e + d, ne)).wait_send()
            return carry

        lax.fori_loop(1, ne, one, 0)

    def part_of(n, q):
        return pl.ds(pl.multiple_of(q * n, 16), n)

    def weight_copy(i, src, dst, q, owner):
        n = src.shape[0]
        return pltpu.make_async_remote_copy(
            src_ref=src,
            dst_ref=dst.at[part_of(n, owner)],
            send_sem=s_w.at[i, q],
            recv_sem=r_w.at[i, owner],
            device_id=(q, e),
            device_id_type=MESH,
        )

    weights = ((wg_ref, wg), (wu_ref, wu), (wd_ref, wd))

    def critic_copies(s, peer, send):
        rt_rows = pl.ds(pl.multiple_of(s * rt, 16), rt)
        big = pltpu.make_async_remote_copy(
            src_ref=ct.at[rt_rows],
            dst_ref=ct.at[rt_rows],
            send_sem=send.at[0],
            recv_sem=r_c.at[0, s],
            device_id=(g, peer),
            device_id_type=MESH,
        )
        small = pltpu.make_async_remote_copy(
            src_ref=cs.at[s],
            dst_ref=cs.at[s],
            send_sem=send.at[1],
            recv_sem=r_c.at[1, s],
            device_id=(g, peer),
            device_id_type=MESH,
        )
        return small, big

    def device(a, b, c):
        return (a * nb + b) * 2 + c

    def two(copies, what):
        for one in copies:
            getattr(one, what)()

    def wider(a, what):
        s = device(a, bb, core)

        def one(d, carry):
            peer = device(aa, lax.rem(bb + d, nb), core)
            two(critic_copies(s, peer, s_c2.at[a, d]), what)
            return carry

        lax.fori_loop(1, nb, one, 0)

    def twin(s, what):
        two(critic_copies(s, device(aa, bb, 1 - core), s_c3.at[s // 2]), what)

    ct[pl.ds(pl.multiple_of(e * rt, 16), rt), :] = ct_ref[...]
    cs[pl.ds(e, 1)] = cs_ref[...][None]

    pl.semaphore_wait(barrier, ne - 1 + ng - 1)

    send_all(outb, routed, s_disp, r_disp)
    for i, (src, dst) in enumerate(weights):

        def one(d, carry):
            weight_copy(i, src, dst, lax.rem(g + d, ng), g).start()
            return carry

        lax.fori_loop(1, ng, one, 0)
        dst[part_of(src.shape[0], g), :] = src[...]

    def stage1(d, what):
        two(critic_copies(e, device(lax.rem(aa + d, na), bb, core), s_c1.at[d]), what)

    def start1(d, carry):
        stage1(d, "start")
        return carry

    lax.fori_loop(1, na, start1, 0)
    wider(aa, "start")
    twin(e, "start")

    take_all(outb, routed, s_disp, r_disp)

    def weights_in(i):
        src, dst = weights[i]

        def one(d, carry):
            q = lax.rem(g + d, ng)
            weight_copy(i, src, dst, q, q).wait_recv()
            return carry

        lax.fori_loop(1, ng, one, 0)

    chunks = 4
    rc = rows // chunks
    per = ne // chunks

    def chunk(i):
        return pl.ds(pl.multiple_of(i * rc, 16), rc)

    weights_in(0)

    def gate_step(i, carry):
        gate[chunk(i), :] = dot(routed[chunk(i), :], wg[...])
        return carry

    lax.fori_loop(0, chunks, gate_step, 0)
    weights_in(1)

    def up_step(i, carry):
        u = dot(routed[chunk(i), :], wu[...])
        up[chunk(i), :] = u
        v = gate[chunk(i), :]
        hid[chunk(i), :] = (v * sigmoid(v) * u).astype(BF)
        return carry

    lax.fori_loop(0, chunks, up_step, 0)
    weights_in(2)

    def down_step(i, carry):
        eout[chunk(i), :] = dot(hid[chunk(i), :], wd[...]).astype(BF)
        return carry

    lax.fori_loop(0, chunks, down_step, 0)
    send_all(eout, back, s_ret, r_ret)

    def pass1(d, carry):
        a = lax.rem(aa + na - d, na)
        s = device(a, bb, core)
        two(critic_copies(s, device(aa, bb, 1 - core), s_c3.at[s // 2]), "wait_recv")
        wider(a, "start")
        twin(s, "start")
        return carry

    lax.fori_loop(1, na, pass1, 0)

    def pass2(j, carry):
        a = lax.rem(aa + na - j // (nb - 1), na)
        b = lax.rem(bb + 1 + lax.rem(j, nb - 1), nb)
        s = device(a, b, core)
        two(critic_copies(s, device(aa, bb, 1 - core), s_c3.at[s // 2]), "wait_recv")
        twin(s, "start")
        return carry

    lax.fori_loop(0, na * (nb - 1), pass2, 0)

    def pass3(j, carry):
        s = j * 2 + 1 - core
        two(critic_copies(s, device(aa, bb, 1 - core), s_c3.at[j]), "wait_recv")
        return carry

    lax.fori_loop(0, na * nb, pass3, 0)

    pre[...] = jnp.zeros_like(pre)
    kc = 1024

    def teach(i, carry):
        cols = pl.ds(pl.multiple_of(i * kc, kc), kc)
        pre[...] += dot(tea_ref[:, cols], ct[cols, :])
        return carry

    lax.fori_loop(0, tea_ref.shape[1] // kc, teach, 0)

    take_all(eout, back, s_ret, r_ret)
    whigh, wlow = split(wslot[...])
    student = (contract_rows(whigh, back[...]) + contract_rows(wlow, back[...])).astype(BF)
    srows = cs[...]
    if srows.shape[1] != rs:
        srows = srows.astype(F32)[:, :rs, :]
    srows = srows.reshape(ne * rs, srows.shape[2]).astype(BF)
    full = pre[...] + dot(student, srows)
    head = ch_ref[...]
    score = jnp.sum(gelu_tanh(full) * head, axis=1, keepdims=True)
    sc_ref[...] = jnp.broadcast_to(score, sc_ref.shape)
    dscore = -jax.nn.sigmoid(-score)
    dpre = (dscore * head * gelu_slope(full)).astype(BF)
    dstudent = contract_cols(dpre, srows)
    dhigh, dlow = split(dstudent)
    sw = jnp.sum(wslot[...], axis=1, keepdims=True)
    gout[...] = (sw * (dot(onehot[...], dhigh) + dot(onehot[...], dlow))).astype(BF)
    send_all(gout, drt, s_dr, r_dr)
    take_all(gout, drt, s_dr, r_dr)

    def grad_copy(i, src, dst, q, owner):
        n = src.shape[0] // ng
        return pltpu.make_async_remote_copy(
            src_ref=src.at[part_of(n, q)],
            dst_ref=dst.at[owner],
            send_sem=s_g.at[i, q],
            recv_sem=r_g.at[i, owner],
            device_id=(q, e),
            device_id_type=MESH,
        )

    grads = ((pd, rd, gd_ref), (pg, rg, gg_ref), (pu, ru, gu_ref))

    def grads_out(i):
        def one(d, carry):
            grad_copy(i, grads[i][0], grads[i][1], lax.rem(g + d, ng), g).start()
            return carry

        lax.fori_loop(1, ng, one, 0)

    def down_grad(i, carry):
        cols = pl.ds(pl.multiple_of(i * 256, 256), 256)
        pd[:, cols] = contract_rows(hid[...], drt[:, cols]).astype(BF)
        return carry

    lax.fori_loop(0, pd.shape[1] // 256, down_grad, 0)
    grads_out(0)

    def hidden_grad(i, carry):
        dh = contract_cols(drt[chunk(i), :], wd[...])
        v = gate[chunk(i), :]
        u = up[chunk(i), :]
        s = sigmoid(v)
        dg[chunk(i), :] = (dh * u * s * (1.0 + v * (1.0 - s))).astype(BF)
        du[chunk(i), :] = (dh * v * s).astype(BF)
        return carry

    lax.fori_loop(0, chunks, hidden_grad, 0)

    for i, (back_ref, part) in enumerate(((dg, pg), (du, pu))):

        def up_grad(j, carry):
            cols = pl.ds(pl.multiple_of(j * 256, 256), 256)
            part[:, cols] = contract_rows(routed[...], back_ref[:, cols]).astype(BF)
            return carry

        lax.fori_loop(0, part.shape[1] // 256, up_grad, 0)
        grads_out(i + 1)

    sent_all(outb, routed, s_disp, r_disp)
    sent_all(eout, back, s_ret, r_ret)
    sent_all(gout, drt, s_dr, r_dr)
    for i, (src, dst) in enumerate(weights):

        def one(d, carry):
            weight_copy(i, src, dst, lax.rem(g + d, ng), g).wait_send()
            return carry

        lax.fori_loop(1, ng, one, 0)

    def end1(d, carry):
        stage1(d, "wait_send")
        return carry

    lax.fori_loop(1, na, end1, 0)

    def end2(a, carry):
        wider(a, "wait_send")
        return carry

    lax.fori_loop(0, na, end2, 0)

    def end3(j, carry):
        twin(j * 2 + core, "wait_send")
        return carry

    lax.fori_loop(0, na * nb, end3, 0)

    for i, (part, got, out) in enumerate(grads):
        n = out.shape[0]
        out[...] = part[part_of(n, g), :].astype(F32)

        def one(d, carry):
            q = lax.rem(g + d, ng)
            copy = grad_copy(i, part, got, q, q)
            copy.wait_recv()
            out[...] += got[q].astype(F32)
            grad_copy(i, part, got, q, g).wait_send()
            return carry

        lax.fori_loop(1, ng, one, 0)


def solution(mesh):
    ng, ne = mesh.shape["grp"], mesh.shape["ep"]
    nb = 2
    while 4 * nb * nb < ne:
        nb *= 2
    na = ne // (2 * nb)

    def step(tokens, teacher, ids, rw, w_gate, w_up, w_down, ct, cs, ch):
        tok, width = tokens.shape
        top = ids.shape[1]
        cap = 3 * tok * top // (2 * ne)
        cap = -(-cap // 16) * 16
        rows = ne * cap
        rs = cs.shape[0]
        rp = -(-rs // 16) * 16
        if rp != rs:
            cs = jnp.pad(cs, ((0, rp - rs), (0, 0)))
        gr, hidden = w_gate.shape[1:]
        dr = w_down.shape[1]
        units = ct.shape[1]
        dma = pltpu.SemaphoreType.DMA
        vm = pl.BlockSpec(memory_space=pltpu.VMEM)
        buf = lambda *s: pltpu.VMEM(s, BF)
        fbuf = lambda *s: pltpu.VMEM(s, F32)
        gg, gu, gd, sc = pl.pallas_call(
            functools.partial(kernel, ng, ne, na, nb, cap, rs),
            out_shape=(
                jax.ShapeDtypeStruct((gr, hidden), F32),
                jax.ShapeDtypeStruct((gr, hidden), F32),
                jax.ShapeDtypeStruct((dr, width), F32),
                jax.ShapeDtypeStruct((tok, 128), F32),
            ),
            in_specs=[vm] * 10,
            out_specs=(vm,) * 4,
            scratch_shapes=[
                buf(ne * ct.shape[0], units),
                buf(ne, rp, units),
                buf(ng * gr, hidden),
                buf(ng * gr, hidden),
                buf(ng * dr, width),
                buf(rows, width),
                buf(rows, width),
                fbuf(rows, hidden),
                fbuf(rows, hidden),
                buf(rows, hidden),
                buf(rows, width),
                buf(rows, width),
                buf(rows, width),
                buf(rows, width),
                buf(rows, hidden),
                buf(rows, hidden),
                buf(ng * gr, hidden),
                buf(ng * gr, hidden),
                buf(ng * dr, width),
                buf(ng, gr, hidden),
                buf(ng, gr, hidden),
                buf(ng, dr, width),
                buf(rows, tok),
                fbuf(rows, tok),
                fbuf(tok, units),
                dma((ne,)),
                dma((ne,)),
                dma((ne,)),
                dma((ne,)),
                dma((ne,)),
                dma((ne,)),
                dma((3, ng)),
                dma((3, ng)),
                dma((3, ng)),
                dma((3, ng)),
                dma((2, ne)),
                dma((na, 2)),
                dma((na, nb, 2)),
                dma((na * nb, 2)),
            ],
            compiler_params=pltpu.CompilerParams(
                collective_id=0, has_side_effects=True, vmem_limit_bytes=56 * 1024 * 1024
            ),
        )(
            tokens,
            teacher,
            ids.T,
            rw.T,
            w_gate[0],
            w_up[0],
            w_down[0],
            ct,
            cs,
            ch[None],
        )
        return gg[None], gu[None], gd[None], sc[:, 0]

    return jax.shard_map(
        step,
        mesh=mesh,
        in_specs=(
            P(("grp", "ep"), None),
            P(("grp", "ep"), None),
            P(("grp", "ep"), None),
            P(("grp", "ep"), None),
            P("ep", "grp", None),
            P("ep", "grp", None),
            P("ep", "grp", None),
            P("ep", None),
            P("ep", None),
            P(),
        ),
        out_specs=(
            P("ep", "grp", None),
            P("ep", "grp", None),
            P("ep", "grp", None),
            P(("grp", "ep")),
        ),
        check_vma=False,
    )
```

```python
import functools

import jax
import jax.numpy as jnp
from jax import lax
from jax.experimental import pallas as pl
from jax.experimental.pallas import tpu as pltpu
from jax.sharding import PartitionSpec as P

BF = jnp.bfloat16
F32 = jnp.float32
MESH = pl.DeviceIdType.MESH


def gelu_tanh(value):
    inner = 0.7978845608 * (value + 0.044715 * value * value * value)
    return 0.5 * value * (1.0 + jnp.tanh(inner))


def gelu_slope(value):
    inner = 0.7978845608 * (value + 0.044715 * value * value * value)
    tangent = jnp.tanh(inner)
    return 0.5 * (1.0 + tangent) + 0.5 * value * (1.0 - tangent * tangent) * 0.7978845608 * (
        1.0 + 3.0 * 0.044715 * value * value
    )


def dot(left, right):
    return jnp.dot(left, right, preferred_element_type=F32)


def contract_rows(left, right):
    return lax.dot_general(left, right, (((0,), (0,)), ((), ())), preferred_element_type=F32)


def contract_cols(left, right):
    return lax.dot_general(left, right, (((1,), (1,)), ((), ())), preferred_element_type=F32)


def split(value):
    high = value.astype(BF)
    return high, (value - high.astype(F32)).astype(BF)


def sigmoid(v):
    return 0.5 * jnp.tanh(0.5 * v) + 0.5


def kernel(
    ng,
    ne,
    na,
    nb,
    cap,
    rs,
    tok_ref,
    tea_ref,
    ids_ref,
    rw_ref,
    wg_ref,
    wu_ref,
    wd_ref,
    ct_ref,
    cs_ref,
    ch_ref,
    gg_ref,
    gu_ref,
    gd_ref,
    sc_ref,
    ct,
    cs,
    wg,
    wu,
    wd,
    outb,
    routed,
    gate,
    up,
    hid,
    eout,
    back,
    gout,
    drt,
    dg,
    du,
    pg,
    pu,
    pd,
    rg,
    ru,
    rd,
    onehot,
    wslot,
    tall,
    tin,
    part,
    pin,
    s_t,
    r_t,
    s_p,
    r_p,
    s_disp,
    r_disp,
    s_ret,
    r_ret,
    s_dr,
    r_dr,
    s_w,
    r_w,
    s_g,
    r_g,
    r_c,
    s_c1,
    s_c2,
    s_c3,
):
    g = lax.axis_index("grp")
    e = lax.axis_index("ep")
    core = lax.rem(e, 2)
    bb = lax.rem(e // 2, nb)
    aa = e // (2 * nb)
    rows = ne * cap
    tok = tok_ref.shape[0]
    rt = ct_ref.shape[0]

    barrier = pltpu.get_barrier_semaphore()

    def greet(d, carry):
        pl.semaphore_signal(
            barrier, inc=1, device_id=(g, lax.rem(e + d, ne)), device_id_type=MESH
        )
        return carry

    lax.fori_loop(1, ne, greet, 0)

    def greet_g(d, carry):
        pl.semaphore_signal(
            barrier, inc=1, device_id=(lax.rem(g + d, ng), e), device_id_type=MESH
        )
        return carry

    lax.fori_loop(1, ng, greet_g, 0)

    row_e = lax.broadcasted_iota(jnp.int32, (ne, tok), 0)
    member = jnp.zeros((ne, tok), F32)
    weight = jnp.zeros((ne, tok), F32)
    for k in range(ids_ref.shape[0]):
        hit = ids_ref[k : k + 1, :] == row_e
        member = jnp.where(hit, 1.0, member)
        weight = jnp.where(hit, rw_ref[k : k + 1, :], weight)
    earlier = (
        lax.broadcasted_iota(jnp.int32, (tok, tok), 0)
        < lax.broadcasted_iota(jnp.int32, (tok, tok), 1)
    ).astype(F32)
    rank = dot(member.astype(BF), earlier.astype(BF))
    rank = jnp.where(member > 0.5, rank, -1.0)
    place = lax.broadcasted_iota(jnp.int32, (ne, cap, tok), 1).astype(F32)
    at = rank[:, None, :] == place
    onehot[...] = jnp.where(at, 1.0, 0.0).reshape(rows, tok).astype(BF)
    wslot[...] = jnp.where(at, weight[:, None, :], 0.0).reshape(rows, tok)
    outb[...] = dot(onehot[...], tok_ref[...]).astype(BF)

    def slots_of(d):
        return pl.ds(pl.multiple_of(d * cap, 16), cap)

    def exchange(src, dst, send, recv, peer):
        return pltpu.make_async_remote_copy(
            src_ref=src.at[slots_of(peer)],
            dst_ref=dst.at[slots_of(e)],
            send_sem=send.at[peer],
            recv_sem=recv.at[e],
            device_id=(g, peer),
            device_id_type=MESH,
        )

    def arrival(src, dst, send, recv, peer):
        return pltpu.make_async_remote_copy(
            src_ref=src.at[slots_of(e)],
            dst_ref=dst.at[slots_of(peer)],
            send_sem=send.at[peer],
            recv_sem=recv.at[peer],
            device_id=(g, peer),
            device_id_type=MESH,
        )

    def send_all(src, dst, send, recv):
        def one(d, carry):
            exchange(src, dst, send, recv, lax.rem(e + d, ne)).start()
            return carry

        lax.fori_loop(1, ne, one, 0)
        dst[slots_of(e), :] = src[slots_of(e), :]

    def take_all(src, dst, send, recv):
        def one(d, carry):
            arrival(src, dst, send, recv, lax.rem(e + ne - d, ne)).wait_recv()
            return carry

        lax.fori_loop(1, ne, one, 0)

    def sent_all(src, dst, send, recv):
        def one(d, carry):
            exchange(src, dst, send, recv, lax.rem(e + d, ne)).wait_send()
            return carry

        lax.fori_loop(1, ne, one, 0)

    def part_of(n, q):
        return pl.ds(pl.multiple_of(q * n, 16), n)

    def weight_copy(i, src, dst, q, owner):
        n = src.shape[0]
        return pltpu.make_async_remote_copy(
            src_ref=src,
            dst_ref=dst.at[part_of(n, owner)],
            send_sem=s_w.at[i, q],
            recv_sem=r_w.at[i, owner],
            device_id=(q, e),
            device_id_type=MESH,
        )

    weights = ((wg_ref, wg), (wu_ref, wu), (wd_ref, wd))

    def critic_copies(s, peer, send):
        rt_rows = pl.ds(pl.multiple_of(s * rt, 16), rt)
        big = pltpu.make_async_remote_copy(
            src_ref=ct.at[rt_rows],
            dst_ref=ct.at[rt_rows],
            send_sem=send.at[0],
            recv_sem=r_c.at[0, s],
            device_id=(g, peer),
            device_id_type=MESH,
        )
        small = pltpu.make_async_remote_copy(
            src_ref=cs.at[s],
            dst_ref=cs.at[s],
            send_sem=send.at[1],
            recv_sem=r_c.at[1, s],
            device_id=(g, peer),
            device_id_type=MESH,
        )
        return small, big

    def device(a, b, c):
        return (a * nb + b) * 2 + c

    def two(copies, what):
        for one in copies:
            getattr(one, what)()

    def wider(a, what):
        s = device(a, bb, core)

        def one(d, carry):
            peer = device(aa, lax.rem(bb + d, nb), core)
            two(critic_copies(s, peer, s_c2.at[a, d])[:1], what)
            return carry

        lax.fori_loop(1, nb, one, 0)

    def twin_copies(s):
        return critic_copies(s, device(aa, bb, 1 - core), s_c3.at[s // 2])

    def twin(s, what):
        two(twin_copies(s), what)

    def block_copy(src, dst, send, recv, b, owner):
        return pltpu.make_async_remote_copy(
            src_ref=src.at[b],
            dst_ref=dst.at[owner],
            send_sem=send.at[b],
            recv_sem=recv.at[owner],
            device_id=(g, device(aa, b, core)),
            device_id_type=MESH,
        )

    def blocks(what, src, dst, send, recv):
        def one(d, carry):
            b = lax.rem(bb + d, nb)
            owner = b if what == "wait_recv" else bb
            getattr(block_copy(src, dst, send, recv, b, owner), what)()
            return carry

        lax.fori_loop(1, nb, one, 0)

    for a in range(na):
        for b in range(nb):
            lo = (a * nb + b) * 2 * rt
            tall[b, a] = tea_ref[:, lo : lo + 2 * rt]
    tin[pl.ds(bb, 1)] = tall[pl.ds(bb, 1)]

    ct[pl.ds(pl.multiple_of(e * rt, 16), rt), :] = ct_ref[...]
    cs[pl.ds(e, 1)] = cs_ref[...][None]

    pl.semaphore_wait(barrier, ne - 1 + ng - 1)

    send_all(outb, routed, s_disp, r_disp)
    for i, (src, dst) in enumerate(weights):

        def one(d, carry):
            weight_copy(i, src, dst, lax.rem(g + d, ng), g).start()
            return carry

        lax.fori_loop(1, ng, one, 0)
        dst[part_of(src.shape[0], g), :] = src[...]

    def hop(a, way, what):
        peer = device(aa + 1 - 2 * way, bb, core)
        two(critic_copies(device(a, bb, core), peer, s_c1.at[a, way]), what)

    def hops(h, what):
        @pl.when((aa - h >= 0) & (aa < na - 1))
        def _():
            hop(aa - h, 0, what)

        @pl.when((aa + h < na) & (aa > 0))
        def _():
            hop(aa + h, 1, what)

    def landed(a):
        s = device(a, bb, core)
        two(twin_copies(s), "wait_recv")
        wider(a, "start")
        twin(s, "start")

    def pass_on(h):
        @pl.when(aa - h >= 0)
        def _():
            landed(aa - h)

        @pl.when(aa + h < na)
        def _():
            landed(aa + h)

        hops(h, "start")

    hops(0, "start")
    wider(aa, "start")
    twin(e, "start")
    blocks("start", tall, tin, s_t, r_t)

    take_all(outb, routed, s_disp, r_disp)
    pass_on(1)

    def weights_in(i):
        src, dst = weights[i]

        def one(d, carry):
            q = lax.rem(g + d, ng)
            weight_copy(i, src, dst, q, q).wait_recv()
            return carry

        lax.fori_loop(1, ng, one, 0)

    chunks = 4
    rc = rows // chunks
    per = ne // chunks

    def chunk(i):
        return pl.ds(pl.multiple_of(i * rc, 16), rc)

    weights_in(0)

    def gate_step(i, carry):
        gate[chunk(i), :] = dot(routed[chunk(i), :], wg[...])
        return carry

    lax.fori_loop(0, chunks, gate_step, 0)
    if na > 2:
        pass_on(2)
    weights_in(1)

    def up_step(i, carry):
        u = dot(routed[chunk(i), :], wu[...])
        up[chunk(i), :] = u
        v = gate[chunk(i), :]
        hid[chunk(i), :] = (v * sigmoid(v) * u).astype(BF)
        return carry

    lax.fori_loop(0, chunks, up_step, 0)
    weights_in(2)

    def down_step(i, carry):
        eout[chunk(i), :] = dot(hid[chunk(i), :], wd[...]).astype(BF)
        return carry

    lax.fori_loop(0, chunks, down_step, 0)
    send_all(eout, back, s_ret, r_ret)

    for h in range(3, na):
        pass_on(h)

    def pass2(j, carry):
        a = lax.rem(aa + na - j // (nb - 1), na)
        b = lax.rem(bb + 1 + lax.rem(j, nb - 1), nb)
        s = device(a, b, core)
        two(twin_copies(s)[:1], "wait_recv")
        two(twin_copies(s)[:1], "start")
        return carry

    def pass3(a, carry):
        two(twin_copies(device(a, bb, 1 - core)), "wait_recv")
        return carry

    lax.fori_loop(0, na, pass3, 0)
    blocks("wait_recv", tall, tin, s_t, r_t)
    tok_all = nb * tok
    part[...] = jnp.zeros_like(part)

    def teach(a, carry):
        mine = pl.ds(pl.multiple_of((a * nb + bb) * 2 * rt, 16), 2 * rt)
        left = tin[:, pl.ds(a, 1)].reshape(tok_all, 2 * rt)
        part[...] += dot(left, ct[mine, :]).reshape(part.shape)
        return carry

    lax.fori_loop(0, na, teach, 0)
    blocks("start", part, pin, s_p, r_p)
    lax.fori_loop(0, na * (nb - 1), pass2, 0)

    def pass4(j, carry):
        a = j // (nb - 1)
        b = lax.rem(bb + 1 + lax.rem(j, nb - 1), nb)
        two(twin_copies(device(a, b, 1 - core))[:1], "wait_recv")
        return carry

    lax.fori_loop(0, na * (nb - 1), pass4, 0)
    pin[pl.ds(bb, 1)] = part[pl.ds(bb, 1)]
    blocks("wait_recv", part, pin, s_p, r_p)

    take_all(eout, back, s_ret, r_ret)
    whigh, wlow = split(wslot[...])
    student = (contract_rows(whigh, back[...]) + contract_rows(wlow, back[...])).astype(BF)
    srows = cs[...]
    if srows.shape[1] != rs:
        srows = srows.astype(F32)[:, :rs, :]
    srows = srows.reshape(ne * rs, srows.shape[2]).astype(BF)
    full = jnp.sum(pin[...], axis=0) + dot(student, srows)
    head = ch_ref[...]
    score = jnp.sum(gelu_tanh(full) * head, axis=1, keepdims=True)
    sc_ref[...] = jnp.broadcast_to(score, sc_ref.shape)
    dscore = -jax.nn.sigmoid(-score)
    dpre = (dscore * head * gelu_slope(full)).astype(BF)
    dstudent = contract_cols(dpre, srows)
    dhigh, dlow = split(dstudent)
    sw = jnp.sum(wslot[...], axis=1, keepdims=True)
    gout[...] = (sw * (dot(onehot[...], dhigh) + dot(onehot[...], dlow))).astype(BF)
    send_all(gout, drt, s_dr, r_dr)
    take_all(gout, drt, s_dr, r_dr)

    def grad_copy(i, src, dst, q, owner):
        n = src.shape[0] // ng
        return pltpu.make_async_remote_copy(
            src_ref=src.at[part_of(n, q)],
            dst_ref=dst.at[owner],
            send_sem=s_g.at[i, q],
            recv_sem=r_g.at[i, owner],
            device_id=(q, e),
            device_id_type=MESH,
        )

    grads = ((pd, rd, gd_ref), (pg, rg, gg_ref), (pu, ru, gu_ref))

    def grads_out(i):
        def one(d, carry):
            grad_copy(i, grads[i][0], grads[i][1], lax.rem(g + d, ng), g).start()
            return carry

        lax.fori_loop(1, ng, one, 0)

    def down_grad(i, carry):
        cols = pl.ds(pl.multiple_of(i * 256, 256), 256)
        pd[:, cols] = contract_rows(hid[...], drt[:, cols]).astype(BF)
        return carry

    lax.fori_loop(0, pd.shape[1] // 256, down_grad, 0)
    grads_out(0)

    def hidden_grad(i, carry):
        dh = contract_cols(drt[chunk(i), :], wd[...])
        v = gate[chunk(i), :]
        u = up[chunk(i), :]
        s = sigmoid(v)
        dg[chunk(i), :] = (dh * u * s * (1.0 + v * (1.0 - s))).astype(BF)
        du[chunk(i), :] = (dh * v * s).astype(BF)
        return carry

    lax.fori_loop(0, chunks, hidden_grad, 0)

    for i, (back_ref, total) in enumerate(((dg, pg), (du, pu))):

        def up_grad(j, carry):
            cols = pl.ds(pl.multiple_of(j * 256, 256), 256)
            total[:, cols] = contract_rows(routed[...], back_ref[:, cols]).astype(BF)
            return carry

        lax.fori_loop(0, total.shape[1] // 256, up_grad, 0)
        grads_out(i + 1)

    sent_all(outb, routed, s_disp, r_disp)
    sent_all(eout, back, s_ret, r_ret)
    sent_all(gout, drt, s_dr, r_dr)
    for i, (src, dst) in enumerate(weights):

        def one(d, carry):
            weight_copy(i, src, dst, lax.rem(g + d, ng), g).wait_send()
            return carry

        lax.fori_loop(1, ng, one, 0)

    for h in range(na):
        hops(h, "wait_send")

    def end2(a, carry):
        wider(a, "wait_send")
        return carry

    lax.fori_loop(0, na, end2, 0)

    def end3(a, carry):
        twin(device(a, bb, core), "wait_send")
        return carry

    lax.fori_loop(0, na, end3, 0)

    def end4(j, carry):
        b = lax.rem(bb + 1 + lax.rem(j, nb - 1), nb)
        two(twin_copies(device(j // (nb - 1), b, core))[:1], "wait_send")
        return carry

    lax.fori_loop(0, na * (nb - 1), end4, 0)
    blocks("wait_send", tall, tin, s_t, r_t)
    blocks("wait_send", part, pin, s_p, r_p)

    for i, (mine, got, out) in enumerate(grads):
        n = out.shape[0]
        out[...] = mine[part_of(n, g), :].astype(F32)

        def one(d, carry):
            q = lax.rem(g + d, ng)
            copy = grad_copy(i, mine, got, q, q)
            copy.wait_recv()
            out[...] += got[q].astype(F32)
            grad_copy(i, mine, got, q, g).wait_send()
            return carry

        lax.fori_loop(1, ng, one, 0)


def solution(mesh):
    ng, ne = mesh.shape["grp"], mesh.shape["ep"]
    nb = 2
    while 4 * nb * nb < ne:
        nb *= 2
    na = ne // (2 * nb)

    def step(tokens, teacher, ids, rw, w_gate, w_up, w_down, ct, cs, ch):
        tok, width = tokens.shape
        top = ids.shape[1]
        cap = 3 * tok * top // (2 * ne)
        cap = -(-cap // 16) * 16
        rows = ne * cap
        rs = cs.shape[0]
        rp = -(-rs // 16) * 16
        if rp != rs:
            cs = jnp.pad(cs, ((0, rp - rs), (0, 0)))
        gr, hidden = w_gate.shape[1:]
        dr = w_down.shape[1]
        units = ct.shape[1]
        dma = pltpu.SemaphoreType.DMA
        vm = pl.BlockSpec(memory_space=pltpu.VMEM)
        buf = lambda *s: pltpu.VMEM(s, BF)
        fbuf = lambda *s: pltpu.VMEM(s, F32)
        gg, gu, gd, sc = pl.pallas_call(
            functools.partial(kernel, ng, ne, na, nb, cap, rs),
            out_shape=(
                jax.ShapeDtypeStruct((gr, hidden), F32),
                jax.ShapeDtypeStruct((gr, hidden), F32),
                jax.ShapeDtypeStruct((dr, width), F32),
                jax.ShapeDtypeStruct((tok, 128), F32),
            ),
            in_specs=[vm] * 10,
            out_specs=(vm,) * 4,
            scratch_shapes=[
                buf(ne * ct.shape[0], units),
                buf(ne, rp, units),
                buf(ng * gr, hidden),
                buf(ng * gr, hidden),
                buf(ng * dr, width),
                buf(rows, width),
                buf(rows, width),
                fbuf(rows, hidden),
                fbuf(rows, hidden),
                buf(rows, hidden),
                buf(rows, width),
                buf(rows, width),
                buf(rows, width),
                buf(rows, width),
                buf(rows, hidden),
                buf(rows, hidden),
                buf(ng * gr, hidden),
                buf(ng * gr, hidden),
                buf(ng * dr, width),
                buf(ng, gr, hidden),
                buf(ng, gr, hidden),
                buf(ng, dr, width),
                buf(rows, tok),
                fbuf(rows, tok),
                buf(nb, na, tok, 2 * ct.shape[0]),
                buf(nb, na, tok, 2 * ct.shape[0]),
                fbuf(nb, tok, units),
                fbuf(nb, tok, units),
                dma((nb,)),
                dma((nb,)),
                dma((nb,)),
                dma((nb,)),
                dma((ne,)),
                dma((ne,)),
                dma((ne,)),
                dma((ne,)),
                dma((ne,)),
                dma((ne,)),
                dma((3, ng)),
                dma((3, ng)),
                dma((3, ng)),
                dma((3, ng)),
                dma((2, ne)),
                dma((na, 2, 2)),
                dma((na, nb, 2)),
                dma((na * nb, 2)),
            ],
            compiler_params=pltpu.CompilerParams(
                collective_id=0, has_side_effects=True, vmem_limit_bytes=56 * 1024 * 1024
            ),
        )(
            tokens,
            teacher,
            ids.T,
            rw.T,
            w_gate[0],
            w_up[0],
            w_down[0],
            ct,
            cs,
            ch[None],
        )
        return gg[None], gu[None], gd[None], sc[:, 0]

    return jax.shard_map(
        step,
        mesh=mesh,
        in_specs=(
            P(("grp", "ep"), None),
            P(("grp", "ep"), None),
            P(("grp", "ep"), None),
            P(("grp", "ep"), None),
            P("ep", "grp", None),
            P("ep", "grp", None),
            P("ep", "grp", None),
            P("ep", None),
            P("ep", None),
            P(),
        ),
        out_specs=(
            P("ep", "grp", None),
            P("ep", "grp", None),
            P("ep", "grp", None),
            P(("grp", "ep")),
        ),
        check_vma=False,
    )
```

```python
import functools

import jax
import jax.numpy as jnp
from jax import lax
from jax.experimental import pallas as pl
from jax.experimental.pallas import tpu as pltpu
from jax.sharding import PartitionSpec as P

BF = jnp.bfloat16
F32 = jnp.float32
MESH = pl.DeviceIdType.MESH


def gelu_tanh(value):
    inner = 0.7978845608 * (value + 0.044715 * value * value * value)
    return 0.5 * value * (1.0 + jnp.tanh(inner))


def gelu_slope(value):
    inner = 0.7978845608 * (value + 0.044715 * value * value * value)
    tangent = jnp.tanh(inner)
    return 0.5 * (1.0 + tangent) + 0.5 * value * (1.0 - tangent * tangent) * 0.7978845608 * (
        1.0 + 3.0 * 0.044715 * value * value
    )


def dot(left, right):
    return jnp.dot(left, right, preferred_element_type=F32)


def contract_rows(left, right):
    return lax.dot_general(left, right, (((0,), (0,)), ((), ())), preferred_element_type=F32)


def contract_cols(left, right):
    return lax.dot_general(left, right, (((1,), (1,)), ((), ())), preferred_element_type=F32)


def split(value):
    high = value.astype(BF)
    return high, (value - high.astype(F32)).astype(BF)


def sigmoid(v):
    return 0.5 * jnp.tanh(0.5 * v) + 0.5


def kernel(
    ng,
    ne,
    na,
    nb,
    cap,
    rs,
    tok_ref,
    tea_ref,
    ids_ref,
    rw_ref,
    wg_ref,
    wu_ref,
    wd_ref,
    ct_ref,
    cs_ref,
    ch_ref,
    gg_ref,
    gu_ref,
    gd_ref,
    sc_ref,
    ct,
    cs,
    wg,
    wu,
    wd,
    outb,
    routed,
    gate,
    up,
    hid,
    eout,
    back,
    gout,
    drt,
    dg,
    du,
    pg,
    pu,
    pd,
    rg,
    ru,
    rd,
    onehot,
    wslot,
    tall,
    tin,
    part,
    pin,
    s_t,
    r_t,
    s_p,
    r_p,
    s_disp,
    r_disp,
    s_ret,
    r_ret,
    s_dr,
    r_dr,
    s_w,
    r_w,
    s_g,
    r_g,
    r_c,
    s_c1,
    s_c2,
    s_c3,
):
    g = lax.axis_index("grp")
    e = lax.axis_index("ep")
    core = lax.rem(e, 2)
    bb = lax.rem(e // 2, nb)
    aa = e // (2 * nb)
    rows = ne * cap
    tok = tok_ref.shape[0]
    rt = ct_ref.shape[0]

    barrier = pltpu.get_barrier_semaphore()

    def greet(d, carry):
        pl.semaphore_signal(
            barrier, inc=1, device_id=(g, lax.rem(e + d, ne)), device_id_type=MESH
        )
        return carry

    lax.fori_loop(1, ne, greet, 0)

    def greet_g(d, carry):
        pl.semaphore_signal(
            barrier, inc=1, device_id=(lax.rem(g + d, ng), e), device_id_type=MESH
        )
        return carry

    lax.fori_loop(1, ng, greet_g, 0)

    row_e = lax.broadcasted_iota(jnp.int32, (ne, tok), 0)
    member = jnp.zeros((ne, tok), F32)
    weight = jnp.zeros((ne, tok), F32)
    for k in range(ids_ref.shape[0]):
        hit = ids_ref[k : k + 1, :] == row_e
        member = jnp.where(hit, 1.0, member)
        weight = jnp.where(hit, rw_ref[k : k + 1, :], weight)
    earlier = (
        lax.broadcasted_iota(jnp.int32, (tok, tok), 0)
        < lax.broadcasted_iota(jnp.int32, (tok, tok), 1)
    ).astype(F32)
    rank = dot(member.astype(BF), earlier.astype(BF))
    rank = jnp.where(member > 0.5, rank, -1.0)
    place = lax.broadcasted_iota(jnp.int32, (ne, cap, tok), 1).astype(F32)
    at = rank[:, None, :] == place
    onehot[...] = jnp.where(at, 1.0, 0.0).reshape(rows, tok).astype(BF)
    wslot[...] = jnp.where(at, weight[:, None, :], 0.0).reshape(rows, tok)
    outb[...] = dot(onehot[...], tok_ref[...]).astype(BF)

    def slots_of(d):
        return pl.ds(pl.multiple_of(d * cap, 16), cap)

    def exchange(src, dst, send, recv, peer):
        return pltpu.make_async_remote_copy(
            src_ref=src.at[slots_of(peer)],
            dst_ref=dst.at[slots_of(e)],
            send_sem=send.at[peer],
            recv_sem=recv.at[e],
            device_id=(g, peer),
            device_id_type=MESH,
        )

    def arrival(src, dst, send, recv, peer):
        return pltpu.make_async_remote_copy(
            src_ref=src.at[slots_of(e)],
            dst_ref=dst.at[slots_of(peer)],
            send_sem=send.at[peer],
            recv_sem=recv.at[peer],
            device_id=(g, peer),
            device_id_type=MESH,
        )

    def send_all(src, dst, send, recv):
        def one(d, carry):
            exchange(src, dst, send, recv, lax.rem(e + d, ne)).start()
            return carry

        lax.fori_loop(1, ne, one, 0)
        dst[slots_of(e), :] = src[slots_of(e), :]

    def take_all(src, dst, send, recv):
        def one(d, carry):
            arrival(src, dst, send, recv, lax.rem(e + ne - d, ne)).wait_recv()
            return carry

        lax.fori_loop(1, ne, one, 0)

    def sent_all(src, dst, send, recv):
        def one(d, carry):
            exchange(src, dst, send, recv, lax.rem(e + d, ne)).wait_send()
            return carry

        lax.fori_loop(1, ne, one, 0)

    def part_of(n, q):
        return pl.ds(pl.multiple_of(q * n, 16), n)

    def weight_copy(i, src, dst, q, owner):
        n = src.shape[0]
        return pltpu.make_async_remote_copy(
            src_ref=src,
            dst_ref=dst.at[part_of(n, owner)],
            send_sem=s_w.at[i, q],
            recv_sem=r_w.at[i, owner],
            device_id=(q, e),
            device_id_type=MESH,
        )

    weights = ((wg_ref, wg), (wu_ref, wu), (wd_ref, wd))

    def critic_copies(s, peer, send):
        rt_rows = pl.ds(pl.multiple_of(s * rt, 16), rt)
        big = pltpu.make_async_remote_copy(
            src_ref=ct.at[rt_rows],
            dst_ref=ct.at[rt_rows],
            send_sem=send.at[0],
            recv_sem=r_c.at[0, s],
            device_id=(g, peer),
            device_id_type=MESH,
        )
        small = pltpu.make_async_remote_copy(
            src_ref=cs.at[s],
            dst_ref=cs.at[s],
            send_sem=send.at[1],
            recv_sem=r_c.at[1, s],
            device_id=(g, peer),
            device_id_type=MESH,
        )
        return small, big

    def device(a, b, c):
        return (a * nb + b) * 2 + c

    def two(copies, what):
        for one in copies:
            getattr(one, what)()

    def wider(a, what):
        s = device(a, bb, core)

        def one(d, carry):
            peer = device(aa, lax.rem(bb + d, nb), core)
            two(critic_copies(s, peer, s_c2.at[a, d])[:1], what)
            return carry

        lax.fori_loop(1, nb, one, 0)

    def twin_copies(s):
        return critic_copies(s, device(aa, bb, 1 - core), s_c3.at[s // 2])

    def twin(s, what):
        two(twin_copies(s), what)

    def block_copy(src, dst, send, recv, b, owner):
        return pltpu.make_async_remote_copy(
            src_ref=src.at[b],
            dst_ref=dst.at[owner],
            send_sem=send.at[b],
            recv_sem=recv.at[owner],
            device_id=(g, device(aa, b, core)),
            device_id_type=MESH,
        )

    def blocks(what, src, dst, send, recv):
        def one(d, carry):
            b = lax.rem(bb + d, nb)
            owner = b if what == "wait_recv" else bb
            getattr(block_copy(src, dst, send, recv, b, owner), what)()
            return carry

        lax.fori_loop(1, nb, one, 0)

    for a in range(na):
        for b in range(nb):
            lo = (a * nb + b) * 2 * rt
            tall[b, a] = tea_ref[:, lo : lo + 2 * rt]
    tin[pl.ds(bb, 1)] = tall[pl.ds(bb, 1)]

    ct[pl.ds(pl.multiple_of(e * rt, 16), rt), :] = ct_ref[...]
    cs[pl.ds(e, 1)] = cs_ref[...][None]

    pl.semaphore_wait(barrier, ne - 1 + ng - 1)

    send_all(outb, routed, s_disp, r_disp)
    for i, (src, dst) in enumerate(weights):

        def one(d, carry):
            weight_copy(i, src, dst, lax.rem(g + d, ng), g).start()
            return carry

        lax.fori_loop(1, ng, one, 0)
        dst[part_of(src.shape[0], g), :] = src[...]

    def hop(a, way, what):
        peer = device(aa + 1 - 2 * way, bb, core)
        two(critic_copies(device(a, bb, core), peer, s_c1.at[a, way]), what)

    def hops(h, what):
        @pl.when((aa - h >= 0) & (aa < na - 1))
        def _():
            hop(aa - h, 0, what)

        @pl.when((aa + h < na) & (aa > 0))
        def _():
            hop(aa + h, 1, what)

    def landed(a):
        s = device(a, bb, core)
        two(twin_copies(s), "wait_recv")
        wider(a, "start")
        twin(s, "start")

    def pass_on(h):
        @pl.when(aa - h >= 0)
        def _():
            landed(aa - h)

        @pl.when(aa + h < na)
        def _():
            landed(aa + h)

        hops(h, "start")

    hops(0, "start")
    wider(aa, "start")
    twin(e, "start")
    blocks("start", tall, tin, s_t, r_t)

    pass_on(1)
    take_all(outb, routed, s_disp, r_disp)

    def weights_in(i):
        src, dst = weights[i]

        def one(d, carry):
            q = lax.rem(g + d, ng)
            weight_copy(i, src, dst, q, q).wait_recv()
            return carry

        lax.fori_loop(1, ng, one, 0)

    chunks = 4
    rc = rows // chunks
    per = ne // chunks

    def chunk(i):
        return pl.ds(pl.multiple_of(i * rc, 16), rc)

    weights_in(0)

    def gate_step(i, carry):
        gate[chunk(i), :] = dot(routed[chunk(i), :], wg[...])
        return carry

    lax.fori_loop(0, chunks, gate_step, 0)
    if na > 2:
        pass_on(2)
    weights_in(1)

    def up_step(i, carry):
        u = dot(routed[chunk(i), :], wu[...])
        up[chunk(i), :] = u
        v = gate[chunk(i), :]
        hid[chunk(i), :] = (v * sigmoid(v) * u).astype(BF)
        return carry

    lax.fori_loop(0, chunks, up_step, 0)
    weights_in(2)

    def down_step(i, carry):
        eout[chunk(i), :] = dot(hid[chunk(i), :], wd[...]).astype(BF)
        return carry

    lax.fori_loop(0, chunks, down_step, 0)
    send_all(eout, back, s_ret, r_ret)

    for h in range(3, na):
        pass_on(h)

    def pass2(j, carry):
        a = lax.rem(aa + na - j // (nb - 1), na)
        b = lax.rem(bb + 1 + lax.rem(j, nb - 1), nb)
        s = device(a, b, core)
        two(twin_copies(s)[:1], "wait_recv")
        two(twin_copies(s)[:1], "start")
        return carry

    def pass3(a, carry):
        two(twin_copies(device(a, bb, 1 - core)), "wait_recv")
        return carry

    lax.fori_loop(0, na, pass3, 0)
    blocks("wait_recv", tall, tin, s_t, r_t)
    tok_all = nb * tok
    part[...] = jnp.zeros_like(part)

    def teach(a, carry):
        mine = pl.ds(pl.multiple_of((a * nb + bb) * 2 * rt, 16), 2 * rt)
        left = tin[:, pl.ds(a, 1)].reshape(tok_all, 2 * rt)
        part[...] += dot(left, ct[mine, :]).reshape(part.shape)
        return carry

    lax.fori_loop(0, na, teach, 0)
    blocks("start", part, pin, s_p, r_p)
    lax.fori_loop(0, na * (nb - 1), pass2, 0)

    def pass4(j, carry):
        a = j // (nb - 1)
        b = lax.rem(bb + 1 + lax.rem(j, nb - 1), nb)
        two(twin_copies(device(a, b, 1 - core))[:1], "wait_recv")
        return carry

    lax.fori_loop(0, na * (nb - 1), pass4, 0)
    pin[pl.ds(bb, 1)] = part[pl.ds(bb, 1)]
    blocks("wait_recv", part, pin, s_p, r_p)

    take_all(eout, back, s_ret, r_ret)
    whigh, wlow = split(wslot[...])
    student = (contract_rows(whigh, back[...]) + contract_rows(wlow, back[...])).astype(BF)
    srows = cs[...]
    if srows.shape[1] != rs:
        srows = srows.astype(F32)[:, :rs, :]
    srows = srows.reshape(ne * rs, srows.shape[2]).astype(BF)
    full = jnp.sum(pin[...], axis=0) + dot(student, srows)
    head = ch_ref[...]
    score = jnp.sum(gelu_tanh(full) * head, axis=1, keepdims=True)
    sc_ref[...] = jnp.broadcast_to(score, sc_ref.shape)
    dscore = -jax.nn.sigmoid(-score)
    dpre = (dscore * head * gelu_slope(full)).astype(BF)
    dstudent = contract_cols(dpre, srows)
    dhigh, dlow = split(dstudent)
    sw = jnp.sum(wslot[...], axis=1, keepdims=True)
    half = gout.shape[1] // 2
    halves = []
    for p in range(2):
        cols = slice(p * half, (p + 1) * half)
        mix = dot(onehot[...], dhigh[:, cols]) + dot(onehot[...], dlow[:, cols])
        gout[:, cols] = (sw * mix).astype(BF)
        halves.append((gout.at[:, cols], drt.at[:, cols], s_dr.at[p], r_dr.at[p]))
        send_all(*halves[p])

    def grad_copy(i, src, dst, q, owner):
        n = src.shape[0] // ng
        return pltpu.make_async_remote_copy(
            src_ref=src.at[part_of(n, q)],
            dst_ref=dst.at[owner],
            send_sem=s_g.at[i, q],
            recv_sem=r_g.at[i, owner],
            device_id=(q, e),
            device_id_type=MESH,
        )

    grads = ((pd, rd, gd_ref), (pg, rg, gg_ref), (pu, ru, gu_ref))

    def down_copy(p, q, owner):
        n = pd.shape[0] // ng
        cols = slice(p * half, (p + 1) * half)
        return pltpu.make_async_remote_copy(
            src_ref=pd.at[part_of(n, q), cols],
            dst_ref=rd.at[owner, :, cols],
            send_sem=s_g.at[3 * p, q],
            recv_sem=r_g.at[3 * p, owner],
            device_id=(q, e),
            device_id_type=MESH,
        )

    def grads_out(i):
        def one(d, carry):
            grad_copy(i, grads[i][0], grads[i][1], lax.rem(g + d, ng), g).start()
            return carry

        lax.fori_loop(1, ng, one, 0)

    for p in range(2):
        take_all(*halves[p])
        cols = slice(p * half, (p + 1) * half)
        pd[:, cols] = contract_rows(hid[...], drt[:, cols]).astype(BF)

        def down_out(d, carry):
            down_copy(p, lax.rem(g + d, ng), g).start()
            return carry

        lax.fori_loop(1, ng, down_out, 0)

    def hidden_grad(i, carry):
        dh = contract_cols(drt[chunk(i), :], wd[...])
        v = gate[chunk(i), :]
        u = up[chunk(i), :]
        s = sigmoid(v)
        dg[chunk(i), :] = (dh * u * s * (1.0 + v * (1.0 - s))).astype(BF)
        du[chunk(i), :] = (dh * v * s).astype(BF)
        return carry

    lax.fori_loop(0, chunks, hidden_grad, 0)

    for i, (back_ref, total) in enumerate(((dg, pg), (du, pu))):

        def up_grad(j, carry):
            cols = pl.ds(pl.multiple_of(j * 256, 256), 256)
            total[:, cols] = contract_rows(routed[...], back_ref[:, cols]).astype(BF)
            return carry

        lax.fori_loop(0, total.shape[1] // 256, up_grad, 0)
        grads_out(i + 1)

    sent_all(outb, routed, s_disp, r_disp)
    sent_all(eout, back, s_ret, r_ret)
    for p in range(2):
        sent_all(*halves[p])
    for i, (src, dst) in enumerate(weights):

        def one(d, carry):
            weight_copy(i, src, dst, lax.rem(g + d, ng), g).wait_send()
            return carry

        lax.fori_loop(1, ng, one, 0)

    for h in range(na):
        hops(h, "wait_send")

    def end2(a, carry):
        wider(a, "wait_send")
        return carry

    lax.fori_loop(0, na, end2, 0)

    def end3(a, carry):
        twin(device(a, bb, core), "wait_send")
        return carry

    lax.fori_loop(0, na, end3, 0)

    def end4(j, carry):
        b = lax.rem(bb + 1 + lax.rem(j, nb - 1), nb)
        two(twin_copies(device(j // (nb - 1), b, core))[:1], "wait_send")
        return carry

    lax.fori_loop(0, na * (nb - 1), end4, 0)
    blocks("wait_send", tall, tin, s_t, r_t)
    blocks("wait_send", part, pin, s_p, r_p)

    for i, (mine, got, out) in enumerate(grads):
        n = out.shape[0]
        out[...] = mine[part_of(n, g), :].astype(F32)

        def one(d, carry):
            q = lax.rem(g + d, ng)
            if i == 0:
                for p in range(2):
                    down_copy(p, q, q).wait_recv()
                    down_copy(p, q, g).wait_send()
            else:
                grad_copy(i, mine, got, q, q).wait_recv()
                grad_copy(i, mine, got, q, g).wait_send()
            out[...] += got[q].astype(F32)
            return carry

        lax.fori_loop(1, ng, one, 0)


def solution(mesh):
    ng, ne = mesh.shape["grp"], mesh.shape["ep"]
    nb = 2
    while 4 * nb * nb < ne:
        nb *= 2
    na = ne // (2 * nb)

    def step(tokens, teacher, ids, rw, w_gate, w_up, w_down, ct, cs, ch):
        tok, width = tokens.shape
        top = ids.shape[1]
        cap = 3 * tok * top // (2 * ne)
        cap = -(-cap // 16) * 16
        rows = ne * cap
        rs = cs.shape[0]
        rp = -(-rs // 16) * 16
        if rp != rs:
            cs = jnp.pad(cs, ((0, rp - rs), (0, 0)))
        gr, hidden = w_gate.shape[1:]
        dr = w_down.shape[1]
        units = ct.shape[1]
        dma = pltpu.SemaphoreType.DMA
        vm = pl.BlockSpec(memory_space=pltpu.VMEM)
        buf = lambda *s: pltpu.VMEM(s, BF)
        fbuf = lambda *s: pltpu.VMEM(s, F32)
        gg, gu, gd, sc = pl.pallas_call(
            functools.partial(kernel, ng, ne, na, nb, cap, rs),
            out_shape=(
                jax.ShapeDtypeStruct((gr, hidden), F32),
                jax.ShapeDtypeStruct((gr, hidden), F32),
                jax.ShapeDtypeStruct((dr, width), F32),
                jax.ShapeDtypeStruct((tok, 128), F32),
            ),
            in_specs=[vm] * 10,
            out_specs=(vm,) * 4,
            scratch_shapes=[
                buf(ne * ct.shape[0], units),
                buf(ne, rp, units),
                buf(ng * gr, hidden),
                buf(ng * gr, hidden),
                buf(ng * dr, width),
                buf(rows, width),
                buf(rows, width),
                fbuf(rows, hidden),
                fbuf(rows, hidden),
                buf(rows, hidden),
                buf(rows, width),
                buf(rows, width),
                buf(rows, width),
                buf(rows, width),
                buf(rows, hidden),
                buf(rows, hidden),
                buf(ng * gr, hidden),
                buf(ng * gr, hidden),
                buf(ng * dr, width),
                buf(ng, gr, hidden),
                buf(ng, gr, hidden),
                buf(ng, dr, width),
                buf(rows, tok),
                fbuf(rows, tok),
                buf(nb, na, tok, 2 * ct.shape[0]),
                buf(nb, na, tok, 2 * ct.shape[0]),
                fbuf(nb, tok, units),
                fbuf(nb, tok, units),
                dma((nb,)),
                dma((nb,)),
                dma((nb,)),
                dma((nb,)),
                dma((ne,)),
                dma((ne,)),
                dma((ne,)),
                dma((ne,)),
                dma((2, ne)),
                dma((2, ne)),
                dma((3, ng)),
                dma((3, ng)),
                dma((4, ng)),
                dma((4, ng)),
                dma((2, ne)),
                dma((na, 2, 2)),
                dma((na, nb, 2)),
                dma((na * nb, 2)),
            ],
            compiler_params=pltpu.CompilerParams(
                collective_id=0, has_side_effects=True, vmem_limit_bytes=56 * 1024 * 1024
            ),
        )(
            tokens,
            teacher,
            ids.T,
            rw.T,
            w_gate[0],
            w_up[0],
            w_down[0],
            ct,
            cs,
            ch[None],
        )
        return gg[None], gu[None], gd[None], sc[:, 0]

    return jax.shard_map(
        step,
        mesh=mesh,
        in_specs=(
            P(("grp", "ep"), None),
            P(("grp", "ep"), None),
            P(("grp", "ep"), None),
            P(("grp", "ep"), None),
            P("ep", "grp", None),
            P("ep", "grp", None),
            P("ep", "grp", None),
            P("ep", None),
            P("ep", None),
            P(),
        ),
        out_specs=(
            P("ep", "grp", None),
            P("ep", "grp", None),
            P("ep", "grp", None),
            P(("grp", "ep")),
        ),
        check_vma=False,
    )
```
